32 devices in a mesh: visit: 4 (over z), sky: 8 (over y, x, core).
Axes of the slice: x: 2, y: 2, z: 4, core: 2. Of those that a mesh axis runs over, the one named last changes fastest.
Arguments:
- cutouts: float32 [64, 512, 512], P(('visit', 'sky')), may hold values from -6 to 6
- vert_taps: float32 [64, 16, 21], P(('visit', 'sky')), may hold values from -1.25 to 1.25
- horiz_taps: float32 [64, 16, 21], P(('visit', 'sky')), may hold values from -1.25 to 1.25
- field_coeffs: float32 [64, 4, 16], P(('visit', 'sky')), may hold values from -1.5 to 1.5
- exposure_weight: float32 [64], P(('visit', 'sky')), may hold values from 0.2 to 2
- dest_owner: int32 [64, 16, 1], P(('visit', 'sky')), may hold values from 0 to 31; in each aligned block of 32 rows (0 to 31, 32 to 63, ..., all dimensions but the last counted through in order) at most 2 rows name the same one
- dest_column: int32 [64, 16], P(('visit', 'sky')), may hold values from 0 to 3
- shift_index: int32 [64, 16], P(('visit', 'sky')), may hold values from 0 to 15
- threshold_level: int32 [32, 4], replicated, may hold values from 1 to 4
Outputs:
- sky_template: float32 [4096, 512], P(('visit', 'sky'))
- difference: float32 [64, 512, 512], P(('visit', 'sky'))
The draws below stay inside these ranges and needn't reach their ends.
Inputs may be any that keep to these rules, and one draw needn't show every extreme that they name: `dest_owner`: among the blocks of the cutouts of one device no owner is named more than 2 times, a bound that some block reaches.
All inputs are finite; a program needn't handle non-finite values.
Results may differ from the reference program's by a relative error of at most 0.0084.
Values may be sent and summed in bfloat16 or wider, within the bound.
A program may use at most 64 MiB of HBM per device.

```python
import math
import jax
import jax.numpy as jnp
import numpy as np
from jax import lax

CUT = 512
BLOCK = 128
KERNELS = 16
TAPS = 21
PW = 4
SHIFTS = 16
SWEEPS = 2
EXP_DEV = 2
BLOCKS = 16
EXPOSURES = 64
OWNERS = 32
CAP = 2
SKY_ROWS = 4096
SKY_COLS = 512
DEVICES = 32


def set_ends(array, key, smallest, largest):
    extent = array.shape
    place = [jax.random.randint(jax.random.fold_in(key, axis), (), 0, extent[axis]) for axis in range(len(extent))]
    array = array.at[tuple(place)].set(smallest)
    longest = extent.index(max(extent))
    place[longest] = (place[longest] + 1) % extent[longest]
    return array.at[tuple(place)].set(largest)


def level_of(key, shape, split, smallest, high):
    def one(dim, shards_of):
        draws = jax.random.uniform(jax.random.fold_in(jax.random.fold_in(key, 6), dim), (shards_of,), jnp.float32, smallest / len(split), high / len(split))
        return jnp.repeat(jnp.exp(draws), shape[dim] // shards_of).reshape((-1,) + (1,) * (len(shape) - dim - 1))

    gain = one(*split[0])
    for cut in split[1:]:
        gain = gain * one(*cut)
    return gain


def deal_out(own_key, own, number, rows, count, top, most, lean):
    sequence = jax.random.permutation(own_key, count)
    heavy_load, common = portions_of(count, rows * top, most, lean, True), portions_of(count, rows * top, most, lean, False)
    places = jnp.arange(count)

    def named(sizes, rotation):
        used = int((sizes > 0).sum())
        fixed = max(1, used // 4)
        moved = fixed + (places - fixed + rotation * (used - fixed)) % max(1, count - fixed)
        return jnp.zeros((count,), jnp.int32).at[sequence[jnp.where(places < fixed, places, moved)]].set(jnp.asarray(sizes, jnp.int32))

    sizes = jnp.where(number % 4 == 0, named(heavy_load, number // 4), named(common, number - number // 4 - 1))
    mixed = jax.random.permutation(jax.random.fold_in(own, 3), count)
    source_of, receiver = mixed[0:count // 2 * 2:2], mixed[1:count // 2 * 2:2]
    slack = jnp.minimum(sizes[source_of] - 1, most - sizes[receiver]) // 2
    slack = jnp.where((source_of == sequence[0]) | (receiver == sequence[0]) | (sizes[receiver] == 0), 0, jnp.maximum(slack, 0))
    moved = jax.random.randint(jax.random.fold_in(own, 4), (count // 2,), 0, 1 << 20) % (slack + 1)
    sizes = sizes.at[source_of].add(-moved).at[receiver].add(moved)
    items = jnp.searchsorted(jnp.cumsum(sizes), jnp.arange(rows * top), side="right").astype(jnp.int32)
    listing = items.reshape(top, rows).T
    listing = listing[jax.random.permutation(jax.random.fold_in(own, 1), rows)]
    rotation = jax.random.randint(jax.random.fold_in(own, 2), (rows, 1), 0, top)
    return jnp.take_along_axis(listing, (jnp.arange(top)[None, :] + rotation) % top, axis=1)


def portions_of(count, total, bound, slope, full):
    weights = [(1 << 20) // math.isqrt(standing ** slope) + 1 for standing in range(1, count + 1)]
    largest = bound if full else min(bound, max(-(-total // count), total * weights[0] // sum(weights)))
    least = 1 if total - largest >= count - 1 else 0
    given, spare = [largest] + [least] * (count - 1), total - largest - least * (count - 1)
    while spare > 0:
        free = [i for i in range(1, count) if given[i] < largest] or [i for i in range(1, count) if given[i] < bound]
        pool, left = sum([weights[i] for i in free]), spare
        for i in free:
            more = min(bound - given[i], max(1, left * weights[i] // pool), spare)
            given[i] = given[i] + more
            spare = spare - more
    return np.array(given)


def centred(rng, shape, width, reach, pieces=(), held_as=jnp.bfloat16):
    gain = level_of(rng, shape, pieces, -0.22, 0.18) if pieces else 1.0
    drawn = jax.random.normal(rng, shape, jnp.float32) * width * gain
    return jnp.minimum(jnp.maximum(drawn, -reach), reach).astype(held_as)


def setup_inputs(seed: int = 0) -> dict:
    key_of = jax.random.split(jax.random.key(seed), 10)
    cutouts = centred(key_of[0], (EXPOSURES, CUT, CUT), 1.0, 6.0, ((0, 32),), jnp.float32)
    vert_taps = centred(key_of[1], (EXPOSURES, KERNELS, TAPS), TAPS ** -0.5, 1.25, ((0, 32),), jnp.float32)
    horiz_taps = centred(key_of[2], (EXPOSURES, KERNELS, TAPS), TAPS ** -0.5, 1.25, ((0, 32),), jnp.float32)
    field_coeffs = centred(key_of[3], (EXPOSURES, 4, KERNELS), KERNELS ** -0.5, 1.5, ((0, 32),), jnp.float32)
    exposure_weight = jnp.clip(jnp.exp(math.log(2.0) - 2.3025851 * jax.random.uniform(key_of[4], (EXPOSURES,), jnp.float32) ** level_of(key_of[4], (EXPOSURES,), ((0, 32),), -0.2, 0.2)), 0.2, 2.0)
    dest_owner_keys = jax.random.split(jax.random.fold_in(key_of[5], 1), EXPOSURES * BLOCKS // (EXP_DEV * BLOCKS))
    dest_owner_turns = jax.random.permutation(jax.random.fold_in(key_of[5], 3), EXPOSURES * BLOCKS // (EXP_DEV * BLOCKS))
    dest_owner = jax.vmap(lambda own, number: deal_out(jax.random.fold_in(key_of[5], 2), own, number, EXP_DEV * BLOCKS, DEVICES, 1, CAP, 2))(dest_owner_keys, dest_owner_turns).reshape((EXPOSURES, BLOCKS, 1))
    dest_column = set_ends(jax.random.randint(key_of[6], (EXPOSURES, BLOCKS), 0, PW), jax.random.fold_in(key_of[6], 1), 0, PW - 1).astype(jnp.int32)
    shift_index = set_ends(jax.random.randint(key_of[7], (EXPOSURES, BLOCKS), 0, SHIFTS), jax.random.fold_in(key_of[7], 1), 0, SHIFTS - 1).astype(jnp.int32)
    threshold_level = set_ends(jax.random.randint(key_of[8], (OWNERS, PW), 1, 5), jax.random.fold_in(key_of[8], 1), 1, 4).astype(jnp.int32)
    return {"cutouts": cutouts, "vert_taps": vert_taps, "horiz_taps": horiz_taps, "field_coeffs": field_coeffs, "exposure_weight": exposure_weight, "dest_owner": dest_owner, "dest_column": dest_column, "shift_index": shift_index, "threshold_level": threshold_level}


highest = lax.Precision.HIGHEST
spline_taps = (0.0625, 0.25, 0.375, 0.25, 0.0625)
fine_tau = 0.04
coarse_tau = 0.02


def to_bf(values):
    return lax.optimization_barrier(values.astype(jnp.bfloat16)).astype(jnp.float32)


def band_matrix(kernel_taps, tile_width):
    margin = (kernel_taps.shape[1] - 1) // 2
    lag_table = jnp.arange(tile_width + 2 * margin)[:, None] - jnp.arange(tile_width)[None, :]
    one_hot = (lag_table[:, :, None] == jnp.arange(kernel_taps.shape[1])[None, None, :]).astype(jnp.float32)
    return jnp.einsum("kt,mnt->kmn", kernel_taps, one_hot, precision=highest)


def convolve_shift(cutout, vertical, horizontal, coeffs, shifts):
    margin = (vertical.shape[1] - 1) // 2
    tile_count = CUT // BLOCK
    window_rows = BLOCK + 2 * margin
    padded = jnp.pad(to_bf(cutout), margin)
    across = band_matrix(to_bf(horizontal), BLOCK)
    downward = band_matrix(to_bf(vertical), BLOCK).transpose(0, 2, 1)
    windows = jnp.stack([padded[:, column_tile * BLOCK:column_tile * BLOCK + window_rows] for column_tile in range(tile_count)])
    col_pos = (jnp.arange(CUT).astype(jnp.float32) + 0.5) / CUT - 0.5

    def row_tile(tile_number):
        window = lax.dynamic_slice_in_dim(windows, tile_number * BLOCK, window_rows, 1)
        smeared = jnp.einsum("tmj,kjn->kmtn", window, across, precision=highest)
        smeared = to_bf(smeared).reshape(KERNELS, window_rows, CUT)
        stacked = jnp.einsum("knm,kmc->knc", downward, smeared, precision=highest)
        basis_parts = jnp.einsum("jk,knc->jnc", coeffs, stacked, precision=highest)
        row_pos = ((tile_number * BLOCK + jnp.arange(BLOCK)).astype(jnp.float32) + 0.5) / CUT - 0.5
        row_pos = row_pos[:, None]
        return basis_parts[0] + row_pos * basis_parts[1] + col_pos[None, :] * basis_parts[2] + (row_pos * col_pos[None, :]) * basis_parts[3]

    convolved = lax.map(row_tile, jnp.arange(tile_count)).reshape(CUT, CUT)
    padded_conv = jnp.pad(convolved, ((0, 1), (0, 1)))
    col_frac = (((shifts % 4).astype(jnp.float32) + 0.5) / 4.0).reshape(tile_count, 1, tile_count, 1)
    row_frac = (((shifts // 4).astype(jnp.float32) + 0.5) / 4.0).reshape(tile_count, 1, tile_count, 1)

    def on_grid(raster):
        return raster.reshape(tile_count, BLOCK, tile_count, BLOCK)

    result = (1.0 - row_frac) * (1.0 - col_frac) * on_grid(convolved)
    result = result + (1.0 - row_frac) * col_frac * on_grid(padded_conv[:-1, 1:])
    result = result + row_frac * (1.0 - col_frac) * on_grid(padded_conv[1:, :-1])
    result = result + row_frac * col_frac * on_grid(padded_conv[1:, 1:])
    return result.transpose(0, 2, 1, 3).reshape(tile_count * tile_count, BLOCK, BLOCK)


def smooth_rows(raster, dilation):
    kept_rows = raster.shape[0] - 4 * dilation
    summed = spline_taps[0] * raster[0:kept_rows]
    for offset in range(1, 5):
        summed = summed + spline_taps[offset] * raster[offset * dilation:offset * dilation + kept_rows]
    return summed


def smooth_cols(raster, dilation):
    col_count = raster.shape[1]
    padded = jnp.pad(raster, ((0, 0), (2 * dilation, 2 * dilation)))
    summed = spline_taps[0] * padded[:, 0:col_count]
    for offset in range(1, 5):
        summed = summed + spline_taps[offset] * padded[:, offset * dilation:offset * dilation + col_count]
    return summed


def shrink(detail, limit):
    return detail - jnp.clip(detail, -limit, limit)


def sweep(raster, limits):
    coarse_one = smooth_cols(smooth_rows(jnp.pad(raster, ((2, 2), (0, 0))), 1), 1)
    coarse_two = smooth_cols(smooth_rows(jnp.pad(coarse_one, ((4, 4), (0, 0))), 2), 2)
    detail_fine = raster - coarse_one
    detail_coarse = coarse_one - coarse_two
    return coarse_two + shrink(detail_fine, fine_tau * limits) + shrink(detail_coarse, coarse_tau * limits)


def reference(cutouts, vert_taps, horiz_taps, field_coeffs, exposure_weight, dest_owner, dest_column, shift_index, threshold_level):
    targets = (dest_owner[:, :, 0] * PW + dest_column).astype(jnp.int32)

    def one_exposure(carry, bundle):
        coadd_sum, weight_total = carry
        cutout, vertical, horizontal, coeffs, weight, target_row, shifts = bundle
        blocks = convolve_shift(cutout, vertical, horizontal, coeffs, shifts)
        weight_bf = to_bf(weight)
        coadd_sum = coadd_sum.at[target_row].add(weight_bf * to_bf(blocks))
        weight_total = weight_total.at[target_row].add(weight_bf * jnp.ones(target_row.shape, jnp.float32))
        return (coadd_sum, weight_total), blocks

    start = (jnp.zeros((OWNERS * PW, BLOCK, BLOCK), jnp.float32), jnp.zeros((OWNERS * PW,), jnp.float32))
    (coadd_sum, weight_total), shifted = lax.scan(one_exposure, start, (cutouts, vert_taps, horiz_taps, field_coeffs, exposure_weight, targets, shift_index))
    coadd = coadd_sum / (1.0 + weight_total)[:, None, None]
    coadd = coadd.reshape(OWNERS, PW, BLOCK, BLOCK).transpose(0, 2, 1, 3).reshape(SKY_ROWS, SKY_COLS)
    levels = threshold_level.astype(jnp.float32)
    limits = jnp.repeat(jnp.repeat(levels, BLOCK, axis=0), BLOCK, axis=1)
    denoised = coadd
    for sweep_number in range(SWEEPS):
        denoised = sweep(denoised, limits)
    template_blocks = to_bf(denoised).reshape(OWNERS, BLOCK, PW, BLOCK).transpose(0, 2, 1, 3).reshape(OWNERS * PW, BLOCK, BLOCK)
    tile_count = CUT // BLOCK

    def difference_of(bundle):
        blocks, target_row = bundle
        raster = blocks - template_blocks[target_row]
        return raster.reshape(tile_count, tile_count, BLOCK, BLOCK).transpose(0, 2, 1, 3).reshape(CUT, CUT)

    difference = lax.map(difference_of, (shifted, targets))
    return denoised, difference
```

```python
import functools
import jax
import jax.numpy as jnp
from jax import lax
from jax.experimental import pallas as pl
from jax.experimental.pallas import tpu as pltpu
from jax.sharding import PartitionSpec as P

BLOCK = 128
PW = 4
SWEEPS = 2
TAIL = 32
TOP = 16

highest = lax.Precision.HIGHEST
spline_taps = (0.0625, 0.25, 0.375, 0.25, 0.0625)
fine_tau = 0.04
coarse_tau = 0.02
reach_rows = 6


def conv_kernel(
    shift_ref,
    owner_ref,
    column_ref,
    weight_ref,
    x_ref,
    across_ref,
    down_ref,
    coef_ref,
    shifted_ref,
    dense_ref,
    padded,
    across,
    band,
    mixing,
    smeared,
    conv,
    conv_right,
):
    exposure = pl.program_id(0)
    side = x_ref.shape[1]
    tiles = side // BLOCK
    kernels = across_ref.shape[1]
    window = BLOCK + TAIL
    wide = side + BLOCK

    @pl.when(exposure == 0)
    def _():
        dense_ref[...] = jnp.zeros_like(dense_ref)

    padded[0:TOP, :] = jnp.zeros((TOP, wide), jnp.bfloat16)
    padded[TOP + side : TOP + side + TOP, :] = jnp.zeros((TOP, wide), jnp.bfloat16)
    for t in range(tiles):
        rows = jnp.concatenate(
            [x_ref[0, t * BLOCK : (t + 1) * BLOCK, :], jnp.zeros((BLOCK, BLOCK), jnp.float32)],
            axis=1,
        )
        padded[TOP + t * BLOCK : TOP + (t + 1) * BLOCK, :] = pltpu.roll(rows, 10, 1).astype(
            jnp.bfloat16
        )

    for k in range(kernels):
        line = jnp.broadcast_to(across_ref[0, k : k + 1, :], (2 * BLOCK, 2 * BLOCK))
        line = pltpu.roll(line, 0, 1, stride=1, stride_axis=0)
        across[:, k * BLOCK : (k + 1) * BLOCK] = line[:, :BLOCK].astype(jnp.bfloat16)
    per = BLOCK // TAIL
    for g in range(kernels // per):
        tail = None
        for q in range(per):
            k = g * per + q
            line = jnp.broadcast_to(down_ref[0, k : k + 1, :], (BLOCK, 2 * BLOCK))
            line = pltpu.roll(line, 0, 1, stride=1, stride_axis=0)
            band[:, k * BLOCK : (k + 1) * BLOCK] = line[:, :BLOCK]
            part = line[:, BLOCK:]
            if q:
                part = pltpu.roll(part, q * TAIL, 1)
            tail = part if tail is None else tail + part
        first = kernels * BLOCK + g * BLOCK
        band[:, first : first + BLOCK] = tail

    lane = lax.broadcasted_iota(jnp.int32, (1, side), 1).astype(jnp.float32)
    v = (lane + 0.5) / side - 0.5

    def row_tile(t, carry):
        first = pl.multiple_of(t * BLOCK, BLOCK)
        stacked = jnp.concatenate(
            [
                padded[pl.ds(first, window), c * BLOCK : (c + 2) * BLOCK]
                for c in range(tiles)
            ],
            axis=0,
        )
        for pair in range(kernels // 2):
            out = jnp.dot(
                stacked,
                across[:, pair * 2 * BLOCK : (pair + 1) * 2 * BLOCK],
                preferred_element_type=jnp.float32,
            ).astype(jnp.bfloat16)
            for half in range(2):
                k = 2 * pair + half
                for c in range(tiles):
                    piece = out[
                        c * window : (c + 1) * window, half * BLOCK : (half + 1) * BLOCK
                    ]
                    lanes = slice(c * BLOCK, (c + 1) * BLOCK)
                    smeared[k * BLOCK : (k + 1) * BLOCK, lanes] = piece[:BLOCK]
                    low = kernels * BLOCK + k * TAIL
                    smeared[low : low + TAIL, lanes] = piece[BLOCK:]
        row = (first + lax.broadcasted_iota(jnp.int32, (BLOCK, 1), 0)).astype(jnp.float32)
        u = (row + 0.5) / side - 0.5
        depth = band.shape[1]
        step = 4 * BLOCK
        for j in range(depth // step):
            s = slice(j * step, (j + 1) * step)
            b = band[:, s]
            c = coef_ref[0, :, s]
            mixing[:BLOCK, s] = ((c[0:1] + u * c[1:2]) * b).astype(jnp.bfloat16)
            mixing[BLOCK:, s] = ((c[2:3] + u * c[3:4]) * b).astype(jnp.bfloat16)
        total = jnp.dot(mixing[...], smeared[...], preferred_element_type=jnp.float32)
        value = total[:BLOCK] + v * total[BLOCK:]
        conv[pl.ds(first, BLOCK), :] = value
        moved = pltpu.roll(value, side - 1, 1)
        conv_right[pl.ds(first, BLOCK), :] = jnp.where(
            lax.broadcasted_iota(jnp.int32, (1, side), 1) < side - 1, moved, 0.0
        )
        return carry

    lax.fori_loop(0, tiles, row_tile, 0)
    conv[side : side + 8, :] = jnp.zeros((8, side), jnp.float32)
    conv_right[side : side + 8, :] = jnp.zeros((8, side), jnp.float32)

    def quarter(number):
        return (number.astype(jnp.float32) + 0.5) / 4.0

    weight = weight_ref[exposure]
    for p in range(tiles):
        for q in range(tiles):
            b = p * tiles + q
            s = shift_ref[exposure, b]
            fx = quarter(lax.rem(s, 4))
            fy = quarter(lax.div(s, 4))
            r = slice(p * BLOCK, (p + 1) * BLOCK)
            below = slice(p * BLOCK + 1, (p + 1) * BLOCK + 1)
            lanes = slice(q * BLOCK, (q + 1) * BLOCK)
            value = (1.0 - fy) * ((1.0 - fx) * conv[r, lanes] + fx * conv_right[r, lanes]) + fy * (
                (1.0 - fx) * conv[below, lanes] + fx * conv_right[below, lanes]
            )
            shifted_ref[0, r, lanes] = value
            sent = weight * value.astype(jnp.bfloat16).astype(jnp.float32)
            at = (
                pl.ds(pl.multiple_of(owner_ref[exposure, b] * BLOCK, BLOCK), BLOCK),
                pl.ds(pl.multiple_of(column_ref[exposure, b] * BLOCK, BLOCK), BLOCK),
            )
            dense_ref[at] = (dense_ref[at].astype(jnp.float32) + sent).astype(jnp.bfloat16)


def difference_kernel(owner_ref, column_ref, shifted_ref, sky_ref, out_ref):
    exposure, p = pl.program_id(0), pl.program_id(1)
    tiles = shifted_ref.shape[2] // BLOCK
    for q in range(tiles):
        b = p * tiles + q
        at = (
            pl.ds(pl.multiple_of(owner_ref[exposure, b] * BLOCK, BLOCK), BLOCK),
            pl.ds(pl.multiple_of(column_ref[exposure, b] * BLOCK, BLOCK), BLOCK),
        )
        lanes = slice(q * BLOCK, (q + 1) * BLOCK)
        out_ref[0, :, lanes] = shifted_ref[0, :, lanes] - sky_ref[at].astype(jnp.float32)


def extended(shard, sides, width):
    for axis, dim in sides:
        peers, length = (lax.axis_size(axis), shard.shape[dim])
        up = [(i, (i + 1) % peers) for i in range(peers - 1)]
        down = [(j, i) for i, j in up]
        last = lax.slice_in_dim(shard, length - width, length, axis=dim)
        leading = lax.slice_in_dim(shard, 0, width, axis=dim)
        before = lax.ppermute(last, axis, up)
        after = lax.ppermute(leading, axis, down)
        shard = jnp.concatenate([before, shard, after], axis=dim)
    return shard


def smooth_rows(raster, dilation):
    kept_rows = raster.shape[0] - 4 * dilation
    summed = spline_taps[0] * raster[0:kept_rows]
    for offset in range(1, 5):
        summed = (
            summed + spline_taps[offset] * raster[offset * dilation : offset * dilation + kept_rows]
        )
    return summed


def smooth_cols(raster, dilation):
    col_count = raster.shape[1]
    padded = jnp.pad(raster, ((0, 0), (2 * dilation, 2 * dilation)))
    summed = spline_taps[0] * padded[:, 0:col_count]
    for offset in range(1, 5):
        summed = (
            summed
            + spline_taps[offset] * padded[:, offset * dilation : offset * dilation + col_count]
        )
    return summed


def shrink(detail, limit):
    return detail - jnp.clip(detail, -limit, limit)


def level_map(first_row, row_count, levels):
    owner_rows = jnp.clip((first_row + jnp.arange(row_count)) // BLOCK, 0, levels.shape[0] - 1)
    one_hot = (owner_rows[:, None] == jnp.arange(levels.shape[0])[None, :]).astype(jnp.float32)
    per_row = jnp.dot(one_hot, levels, precision=highest)
    return jnp.repeat(per_row, BLOCK, axis=1)


def sweep(wide, first_row, levels, sky_rows):
    row_count = wide.shape[0]
    positions = first_row + jnp.arange(row_count)
    inside = ((positions >= 0) & (positions < sky_rows)).astype(jnp.float32)[:, None]
    coarse_zero = wide * inside
    coarse_one = smooth_cols(smooth_rows(coarse_zero, 1), 1) * inside[2 : row_count - 2]
    coarse_two = smooth_cols(smooth_rows(coarse_one, 2), 2)
    kept_rows = row_count - 12
    detail_fine = coarse_zero[6 : 6 + kept_rows] - coarse_one[4 : 4 + kept_rows]
    detail_coarse = coarse_one[4 : 4 + kept_rows] - coarse_two
    limits = level_map(first_row + 6, kept_rows, levels)
    return (
        coarse_two
        + shrink(detail_fine, fine_tau * limits)
        + shrink(detail_coarse, coarse_tau * limits)
    )


def bf_values(array):
    return array.astype(jnp.bfloat16).astype(jnp.float32)


def shards(
    cutouts,
    vert_taps,
    horiz_taps,
    field_coeffs,
    exposure_weight,
    dest_owner,
    dest_column,
    shift_index,
    threshold_level,
):
    exposures, side, _ = cutouts.shape
    tiles = side // BLOCK
    kernels, taps = vert_taps.shape[1:]
    axes = ("visit", "sky")
    devices = lax.axis_size("visit") * lax.axis_size("sky")
    sky_rows = devices * BLOCK
    sky_cols = PW * BLOCK
    owners = dest_owner.reshape(exposures, tiles * tiles)
    weight = bf_values(exposure_weight)

    targets = owners * PW + dest_column
    hits = (targets[:, :, None] == jnp.arange(devices * PW)[None, None, :]).astype(jnp.float32)
    own_weights = jnp.sum(hits * weight[:, None, None], axis=(0, 1))
    all_weights = lax.all_gather(own_weights, axes)
    me = lax.axis_index(axes)
    total_weight = lax.dynamic_slice_in_dim(jnp.sum(all_weights, axis=0), me * PW, PW)

    horizontal, vertical = bf_values(horiz_taps), bf_values(vert_taps)
    gap = 2 * BLOCK - taps
    across_rows = jnp.concatenate(
        [
            horizontal[:, :, :1],
            jnp.zeros((exposures, kernels, gap), jnp.float32),
            horizontal[:, :, :0:-1],
        ],
        axis=2,
    )
    margin = (taps - 1) // 2
    down_rows = jnp.pad(
        vertical, ((0, 0), (0, 0), (TOP - margin, gap - (TOP - margin)))
    )
    coef_lanes = jnp.concatenate(
        [jnp.repeat(field_coeffs, BLOCK, axis=2), jnp.repeat(field_coeffs, TAIL, axis=2)], axis=2
    )
    depth = kernels * (BLOCK + TAIL)
    shifted, dense = pl.pallas_call(
        conv_kernel,
        grid_spec=pltpu.PrefetchScalarGridSpec(
            num_scalar_prefetch=4,
            grid=(exposures,),
            in_specs=[
                pl.BlockSpec((1, side, side), lambda e, *_: (e, 0, 0)),
                pl.BlockSpec((1, kernels, 2 * BLOCK), lambda e, *_: (e, 0, 0)),
                pl.BlockSpec((1, kernels, 2 * BLOCK), lambda e, *_: (e, 0, 0)),
                pl.BlockSpec((1, 4, depth), lambda e, *_: (e, 0, 0)),
            ],
            out_specs=[
                pl.BlockSpec((1, side, side), lambda e, *_: (e, 0, 0)),
                pl.BlockSpec((sky_rows, sky_cols), lambda e, *_: (0, 0)),
            ],
            scratch_shapes=[
                pltpu.VMEM((side + 2 * TOP, side + BLOCK), jnp.bfloat16),
                pltpu.VMEM((2 * BLOCK, kernels * BLOCK), jnp.bfloat16),
                pltpu.VMEM((BLOCK, depth), jnp.float32),
                pltpu.VMEM((2 * BLOCK, depth), jnp.bfloat16),
                pltpu.VMEM((depth, side), jnp.bfloat16),
                pltpu.VMEM((side + 8, side), jnp.float32),
                pltpu.VMEM((side + 8, side), jnp.float32),
            ],
        ),
        out_shape=[
            jax.ShapeDtypeStruct((exposures, side, side), jnp.float32),
            jax.ShapeDtypeStruct((sky_rows, sky_cols), jnp.bfloat16),
        ],
        compiler_params=pltpu.CompilerParams(vmem_limit_bytes=56 * 1024 * 1024),
        name="convolve",
    )(shift_index, owners, dest_column, weight, cutouts, across_rows, down_rows, coef_lanes)

    summed = lax.psum_scatter(dense, axes, scatter_dimension=0, tiled=True)
    scale = jnp.repeat(1.0 + total_weight, BLOCK)[None, :]
    strip = summed.astype(jnp.float32) / scale
    levels = threshold_level.astype(jnp.float32)
    first_row = me * BLOCK
    wide = extended(strip, ((axes, 0),), SWEEPS * reach_rows)
    for sweep_number in range(SWEEPS):
        wide = sweep(wide, first_row - (SWEEPS - sweep_number) * reach_rows, levels, sky_rows)
    strip = wide
    sky = lax.all_gather(strip.astype(jnp.bfloat16), axes, axis=0, tiled=True)

    difference = pl.pallas_call(
        difference_kernel,
        grid_spec=pltpu.PrefetchScalarGridSpec(
            num_scalar_prefetch=2,
            grid=(exposures, tiles),
            in_specs=[
                pl.BlockSpec((1, BLOCK, side), lambda e, p, *_: (e, p, 0)),
                pl.BlockSpec((sky_rows, sky_cols), lambda e, p, *_: (0, 0)),
            ],
            out_specs=pl.BlockSpec((1, BLOCK, side), lambda e, p, *_: (e, p, 0)),
        ),
        out_shape=jax.ShapeDtypeStruct((exposures, side, side), jnp.float32),
        compiler_params=pltpu.CompilerParams(vmem_limit_bytes=56 * 1024 * 1024),
        name="difference",
    )(owners, dest_column, shifted, sky)
    return (strip, difference)


def solution(mesh):
    placed = (
        P(("visit", "sky"), None, None),
        P(("visit", "sky"), None, None),
        P(("visit", "sky"), None, None),
        P(("visit", "sky"), None, None),
        P(("visit", "sky")),
        P(("visit", "sky"), None, None),
        P(("visit", "sky"), None),
        P(("visit", "sky"), None),
        P(),
    )
    return jax.shard_map(
        shards,
        mesh=mesh,
        in_specs=placed,
        out_specs=(P(("visit", "sky"), None), P(("visit", "sky"), None, None)),
        check_vma=False,
    )
```

```python
import functools
import jax
import jax.numpy as jnp
from jax import lax
from jax.experimental import pallas as pl
from jax.experimental.pallas import tpu as pltpu
from jax.sharding import PartitionSpec as P

BLOCK = 128
PW = 4
SWEEPS = 2
TAIL = 32
TOP = 16

spline_taps = (0.0625, 0.25, 0.375, 0.25, 0.0625)
fine_tau = 0.04
coarse_tau = 0.02


def bf_values(array):
    return array.astype(jnp.bfloat16).astype(jnp.float32)


def conv_kernel(
    shift_ref,
    owner_ref,
    column_ref,
    weight_ref,
    factor_ref,
    x_ref,
    across_ref,
    down_ref,
    shifted_ref,
    dense_ref,
    total_ref,
    padded,
    tap_rows,
    coef,
    across,
    band,
    mixing,
    smeared,
    conv,
    conv_right,
):
    exposure = pl.program_id(0)
    side = x_ref.shape[1]
    tiles = side // BLOCK
    kernels = across_ref.shape[1]
    window = BLOCK + TAIL
    wide = side + BLOCK

    @pl.when(exposure == 0)
    def _():
        dense_ref[...] = jnp.zeros_like(dense_ref)
        total_ref[...] = jnp.zeros_like(total_ref)

    padded[0:TOP, :] = jnp.zeros((TOP, wide), jnp.bfloat16)
    padded[TOP + side : TOP + side + TOP, :] = jnp.zeros((TOP, wide), jnp.bfloat16)
    for t in range(tiles):
        rows = jnp.concatenate(
            [x_ref[0, t * BLOCK : (t + 1) * BLOCK, :], jnp.zeros((BLOCK, BLOCK), jnp.float32)],
            axis=1,
        )
        padded[TOP + t * BLOCK : TOP + (t + 1) * BLOCK, :] = pltpu.roll(rows, 10, 1).astype(
            jnp.bfloat16
        )

    taps = across_ref.shape[2]
    margin = (taps - 1) // 2
    source = lax.broadcasted_iota(jnp.int32, (BLOCK, 2 * BLOCK), 0)
    place = lax.broadcasted_iota(jnp.int32, (BLOCK, 2 * BLOCK), 1)
    backward = (place == lax.rem(2 * BLOCK - source, 2 * BLOCK)) & (source < taps)
    forward = (place == source + (TOP - margin)) & (source < taps)

    def lined(taps_ref, at):
        tap_rows[...] = jnp.zeros_like(tap_rows)
        tap_rows[:, :taps] = taps_ref[0]
        return jnp.dot(
            tap_rows[...].astype(jnp.bfloat16),
            at.astype(jnp.float32).astype(jnp.bfloat16),
            preferred_element_type=jnp.float32,
        )

    across_lines = lined(across_ref, backward)
    down_lines = lined(down_ref, forward)
    quarter_of = lax.broadcasted_iota(jnp.int32, (1, BLOCK), 1) // TAIL
    for j in range(4):
        for k in range(kernels):
            coef[j : j + 1, k * BLOCK : (k + 1) * BLOCK] = jnp.full(
                (1, BLOCK), factor_ref[exposure, j, k]
            )
        for g in range(kernels * TAIL // BLOCK):
            row = jnp.zeros((1, BLOCK), jnp.float32)
            for q in range(BLOCK // TAIL):
                row = jnp.where(
                    quarter_of == q, factor_ref[exposure, j, g * (BLOCK // TAIL) + q], row
                )
            low = kernels * BLOCK + g * BLOCK
            coef[j : j + 1, low : low + BLOCK] = row

    for k in range(kernels):
        line = jnp.broadcast_to(across_lines[k : k + 1, :], (2 * BLOCK, 2 * BLOCK))
        line = pltpu.roll(line, 0, 1, stride=1, stride_axis=0)
        across[:, k * BLOCK : (k + 1) * BLOCK] = line[:, :BLOCK].astype(jnp.bfloat16)
    per = BLOCK // TAIL
    for g in range(kernels // per):
        tail = None
        for q in range(per):
            k = g * per + q
            line = jnp.broadcast_to(down_lines[k : k + 1, :], (BLOCK, 2 * BLOCK))
            line = pltpu.roll(line, 0, 1, stride=1, stride_axis=0)
            band[:, k * BLOCK : (k + 1) * BLOCK] = line[:, :BLOCK]
            part = line[:, BLOCK:]
            if q:
                part = pltpu.roll(part, q * TAIL, 1)
            tail = part if tail is None else tail + part
        first = kernels * BLOCK + g * BLOCK
        band[:, first : first + BLOCK] = tail

    lane = lax.broadcasted_iota(jnp.int32, (1, side), 1).astype(jnp.float32)
    v = (lane + 0.5) / side - 0.5

    def row_tile(t, carry):
        first = pl.multiple_of(t * BLOCK, BLOCK)
        stacked = jnp.concatenate(
            [
                padded[pl.ds(first, window), c * BLOCK : (c + 2) * BLOCK]
                for c in range(tiles)
            ],
            axis=0,
        )
        for pair in range(kernels // 2):
            out = jnp.dot(
                stacked,
                across[:, pair * 2 * BLOCK : (pair + 1) * 2 * BLOCK],
                preferred_element_type=jnp.float32,
            ).astype(jnp.bfloat16)
            for half in range(2):
                k = 2 * pair + half
                for c in range(tiles):
                    piece = out[
                        c * window : (c + 1) * window, half * BLOCK : (half + 1) * BLOCK
                    ]
                    lanes = slice(c * BLOCK, (c + 1) * BLOCK)
                    smeared[k * BLOCK : (k + 1) * BLOCK, lanes] = piece[:BLOCK]
                    low = kernels * BLOCK + k * TAIL
                    smeared[low : low + TAIL, lanes] = piece[BLOCK:]
        row = (first + lax.broadcasted_iota(jnp.int32, (BLOCK, 1), 0)).astype(jnp.float32)
        u = (row + 0.5) / side - 0.5
        depth = band.shape[1]
        step = 4 * BLOCK
        for j in range(depth // step):
            s = slice(j * step, (j + 1) * step)
            b = band[:, s]
            c = coef[:, s]
            mixing[:BLOCK, s] = ((c[0:1] + u * c[1:2]) * b).astype(jnp.bfloat16)
            mixing[BLOCK:, s] = ((c[2:3] + u * c[3:4]) * b).astype(jnp.bfloat16)
        total = jnp.dot(mixing[...], smeared[...], preferred_element_type=jnp.float32)
        value = total[:BLOCK] + v * total[BLOCK:]
        conv[pl.ds(first, BLOCK), :] = value
        moved = pltpu.roll(value, side - 1, 1)
        conv_right[pl.ds(first, BLOCK), :] = jnp.where(
            lax.broadcasted_iota(jnp.int32, (1, side), 1) < side - 1, moved, 0.0
        )
        return carry

    lax.fori_loop(0, tiles, row_tile, 0)
    conv[side : side + 8, :] = jnp.zeros((8, side), jnp.float32)
    conv_right[side : side + 8, :] = jnp.zeros((8, side), jnp.float32)

    def quarter(number):
        return (number.astype(jnp.float32) + 0.5) / 4.0

    weight = bf_values(jnp.full((8, BLOCK), weight_ref[exposure]))
    lanes_of = lax.broadcasted_iota(jnp.int32, (8, BLOCK), 1)
    for p in range(tiles):
        for q in range(tiles):
            b = p * tiles + q
            s = shift_ref[exposure, b]
            fx = quarter(lax.rem(s, 4))
            fy = quarter(lax.div(s, 4))
            r = slice(p * BLOCK, (p + 1) * BLOCK)
            below = slice(p * BLOCK + 1, (p + 1) * BLOCK + 1)
            lanes = slice(q * BLOCK, (q + 1) * BLOCK)
            value = (1.0 - fy) * ((1.0 - fx) * conv[r, lanes] + fx * conv_right[r, lanes]) + fy * (
                (1.0 - fx) * conv[below, lanes] + fx * conv_right[below, lanes]
            )
            shifted_ref[0, r, lanes] = value
            sent = weight[0:1] * value.astype(jnp.bfloat16).astype(jnp.float32)
            at = (
                pl.ds(pl.multiple_of(owner_ref[exposure, b] * BLOCK, BLOCK), BLOCK),
                pl.ds(pl.multiple_of(column_ref[exposure, b] * BLOCK, BLOCK), BLOCK),
            )
            owner = owner_ref[exposure, b]
            total_ref[owner] = total_ref[owner] + jnp.where(
                lanes_of == column_ref[exposure, b], weight, 0.0
            )
            dense_ref[at] = (dense_ref[at].astype(jnp.float32) + sent).astype(jnp.bfloat16)


def difference_kernel(owner_ref, column_ref, shifted_ref, sky_ref, out_ref, blocks, sems):
    exposure, p = pl.program_id(0), pl.program_id(1)
    tiles = shifted_ref.shape[2] // BLOCK
    exposures = owner_ref.shape[0]

    def fetch(e, b):
        source = sky_ref.at[
            pl.ds(pl.multiple_of(owner_ref[e, b] * BLOCK, BLOCK), BLOCK),
            pl.ds(pl.multiple_of(column_ref[e, b] * BLOCK, BLOCK), BLOCK),
        ]
        return pltpu.make_async_copy(source, blocks.at[e, b], sems.at[e, b])

    @pl.when((exposure == 0) & (p == 0))
    def _():
        for e in range(exposures):
            for b in range(tiles * tiles):
                fetch(e, b).start()

    for q in range(tiles):
        b = p * tiles + q
        fetch(exposure, b).wait()
        lanes = slice(q * BLOCK, (q + 1) * BLOCK)
        out_ref[0, :, lanes] = shifted_ref[0, :, lanes] - blocks[exposure, b].astype(jnp.float32)


def spline(values, dilation, axis):
    size = values.shape[axis]
    d = dilation
    near = pltpu.roll(values, d, axis) + pltpu.roll(values, size - d, axis)
    far = pltpu.roll(values, 2 * d, axis) + pltpu.roll(values, size - 2 * d, axis)
    return spline_taps[0] * far + spline_taps[1] * near + spline_taps[2] * values


def shrink(detail, limit):
    return detail - jnp.minimum(jnp.maximum(detail, -limit), limit)


def smooth(values, dilation):
    rows, cols = values.shape
    down = spline(values, dilation, 0)
    wide = jnp.concatenate([down, jnp.zeros((rows, BLOCK), jnp.float32)], axis=1)
    return spline(wide, dilation, 1)[:, :cols]


def combine_kernel(
    visits,
    pairs,
    dense_ref,
    weight_ref,
    level_ref,
    strip_ref,
    sky_ref,
    part,
    from_twin,
    from_plane,
    going,
    from_visit,
    w_part,
    w_twin,
    w_plane,
    w_going,
    w_visit,
    edges,
    halo,
    template,
    local_sem,
    twin_sem,
    plane_sem,
    visit_sem,
    w_sem,
    halo_sem,
    back_visit_sem,
    back_plane_sem,
    back_twin_sem,
):
    z = lax.axis_index("visit")
    sky = lax.axis_index("sky")
    peers = 2 * pairs
    devices = visits * peers
    p, core = lax.div(sky, 2), lax.rem(sky, 2)
    me = z * peers + sky
    other = 1 - core

    def linear(number):
        return (lax.div(number, peers), lax.rem(number, peers))

    twin = (z, p * 2 + other)
    places = [lax.rem(p + o, pairs) for o in range(1, pairs)]
    plane = [(z, place * 2 + core) for place in places]
    heights = [lax.rem(z + d, visits) for d in range(1, visits)]
    column = [(height, sky) for height in heights]
    ring = [linear(lax.rem(me + devices - 1, devices)), linear(lax.rem(me + 1, devices))]

    everyone = [twin] + plane + column + ring
    barrier = pltpu.get_barrier_semaphore()
    for peer in everyone:
        pl.semaphore_signal(
            barrier, inc=1, device_id=peer, device_id_type=pl.DeviceIdType.MESH
        )
    pl.semaphore_wait(barrier, len(everyone))

    def send(src, dst, sems, index, peer):
        copy = pltpu.make_async_remote_copy(
            src_ref=src,
            dst_ref=dst,
            send_sem=sems.at[(0,) + index],
            recv_sem=sems.at[(1,) + index],
            device_id=peer,
            device_id_type=pl.DeviceIdType.MESH,
        )
        copy.start()
        sent.append(copy)
        return copy

    sent = []
    order = heights + [z]
    w_copy = send(weight_ref.at[:, :, other], w_twin, w_sem, (0,), twin)
    local, across = [], []
    for j, height in enumerate(order):
        across.append(
            send(dense_ref.at[height, :, other], from_twin.at[j], twin_sem, (j,), twin)
        )
        own = pltpu.make_async_copy(dense_ref.at[height, :, core], part.at[j], local_sem.at[j])
        own.start()
        local.append(own)

    w_copy.wait_recv()
    for height in range(visits):
        for place in range(pairs):
            w_part[place, height] = weight_ref[height, place, core] + w_twin[height, place]
    w_copies = [
        send(w_part.at[place], w_plane.at[o], w_sem, (1 + o,), plane[o])
        for o, place in enumerate(places)
    ]

    def spread(j):
        local[j].wait()
        across[j].wait_recv()

        def add(place, carry):
            part[j, place] = (
                part[j, place].astype(jnp.float32) + from_twin[j, place].astype(jnp.float32)
            ).astype(jnp.bfloat16)
            return carry

        lax.fori_loop(0, pairs, add, 0)
        return [
            send(part.at[j, place], from_plane.at[j, o], plane_sem, (j, o), plane[o])
            for o, place in enumerate(places)
        ]

    def gathered(j):
        total = part[j, p].astype(jnp.float32)
        for o in range(pairs - 1):
            total = total + from_plane[j, o].astype(jnp.float32)
        return total

    moves = [spread(0)]
    for copy in w_copies:
        copy.wait_recv()
    w_total = w_part[p]
    for o in range(pairs - 1):
        w_total = w_total + w_plane[o]
    w_going[...] = w_total
    w_copies = [
        send(w_going.at[height], w_visit.at[j], w_sem, (pairs + j,), column[j])
        for j, height in enumerate(heights)
    ]
    climbs = []
    for j in range(visits):
        if j + 1 < visits:
            moves.append(spread(j + 1))
        for copy in moves[j]:
            copy.wait_recv()
        if j + 1 < visits:
            going[j] = gathered(j).astype(jnp.bfloat16)
            climbs.append(send(going.at[j], from_visit.at[j], visit_sem, (j,), column[j]))
    weight = w_going[z]
    for copy, j in zip(w_copies, range(visits - 1)):
        copy.wait_recv()
        weight = weight + w_visit[j]
    total = gathered(visits - 1)
    for copy, j in zip(climbs, range(visits - 1)):
        copy.wait_recv()
        total = total + from_visit[j].astype(jnp.float32)
    cols = total.shape[1]
    blocks = cols // BLOCK
    scale = jnp.concatenate(
        [jnp.broadcast_to(1.0 + weight[0:1, c : c + 1], (1, BLOCK)) for c in range(blocks)], axis=1
    )
    coadd = total / scale
    edges[0] = coadd[:TOP]
    edges[1] = coadd[BLOCK - TOP :]
    shifts = [
        send(edges.at[0], halo.at[1], halo_sem, (0,), ring[0]),
        send(edges.at[1], halo.at[0], halo_sem, (1,), ring[1]),
    ]
    for copy in shifts:
        copy.wait_recv()

    rows = BLOCK + 2 * TOP
    position = me * BLOCK - TOP + lax.broadcasted_iota(jnp.int32, (rows, 1), 0)
    inside = jnp.where((position >= 0) & (position < devices * BLOCK), 1.0, 0.0)
    above, below = jnp.maximum(me - 1, 0), jnp.minimum(me + 1, devices - 1)

    def levels(owner, height):
        row = level_ref[pl.ds(owner, 1), :].astype(jnp.float32)
        return jnp.concatenate(
            [
                jnp.broadcast_to(row[:, c : c + 1], (height, BLOCK))
                for c in range(blocks)
            ],
            axis=1,
        )

    limits = jnp.concatenate([levels(above, TOP), levels(me, BLOCK), levels(below, TOP)], axis=0)
    values = jnp.concatenate([halo[0], coadd, halo[1]], axis=0)
    for _ in range(SWEEPS):
        values = values * inside
        fine = smooth(values, 1) * inside
        coarse = smooth(fine, 2)
        values = (
            coarse
            + shrink(values - fine, fine_tau * limits)
            + shrink(fine - coarse, coarse_tau * limits)
        )
    strip = values[TOP : TOP + BLOCK]
    strip_ref[...] = strip
    template[...] = strip.astype(jnp.bfloat16)

    mine = sky_ref.at[z, p, core]
    own = pltpu.make_async_copy(template, mine, local_sem.at[visits])
    own.start()
    climbs = [
        send(template, mine, back_visit_sem, (d,), column[d]) for d in range(visits - 1)
    ]
    spreads, twins = [], []

    def outward(d):
        if d == 0:
            source, place = template, mine
        else:
            climbs[d - 1].wait_recv()
            source = place = sky_ref.at[lax.rem(z + visits - d, visits), p, core]
        spreads.append(
            [send(source, place, back_plane_sem, (d, o), plane[o]) for o in range(pairs - 1)]
        )
        twins.append(send(source, place, back_twin_sem, (d, pairs - 1), twin))

    outward(0)
    for d in range(visits):
        if d + 1 < visits:
            outward(d + 1)
        for o in range(pairs - 1):
            spreads[d][o].wait_recv()
            place = sky_ref.at[
                lax.rem(z + visits - d, visits), lax.rem(p + pairs - 1 - o, pairs), core
            ]
            twins.append(send(place, place, back_twin_sem, (d, o), twin))
    for copy in twins:
        copy.wait_recv()
    own.wait()
    for copy in sent:
        copy.wait_send()


def shards(
    cutouts,
    vert_taps,
    horiz_taps,
    field_coeffs,
    exposure_weight,
    dest_owner,
    dest_column,
    shift_index,
    threshold_level,
):
    exposures, side, _ = cutouts.shape
    tiles = side // BLOCK
    kernels, taps = vert_taps.shape[1:]
    axes = ("visit", "sky")
    devices = lax.axis_size("visit") * lax.axis_size("sky")
    sky_rows = devices * BLOCK
    sky_cols = PW * BLOCK
    owners = dest_owner.reshape(exposures, tiles * tiles)

    depth = kernels * (BLOCK + TAIL)
    shifted, dense, weights = pl.pallas_call(
        conv_kernel,
        grid_spec=pltpu.PrefetchScalarGridSpec(
            num_scalar_prefetch=5,
            grid=(exposures,),
            in_specs=[
                pl.BlockSpec((1, side, side), lambda e, *_: (e, 0, 0)),
                pl.BlockSpec((1, kernels, taps), lambda e, *_: (e, 0, 0)),
                pl.BlockSpec((1, kernels, taps), lambda e, *_: (e, 0, 0)),
            ],
            out_specs=[
                pl.BlockSpec((1, side, side), lambda e, *_: (e, 0, 0)),
                pl.BlockSpec((sky_rows, sky_cols), lambda e, *_: (0, 0)),
                pl.BlockSpec((devices, 8, BLOCK), lambda e, *_: (0, 0, 0)),
            ],
            scratch_shapes=[
                pltpu.VMEM((side + 2 * TOP, side + BLOCK), jnp.bfloat16),
                pltpu.VMEM((kernels, BLOCK), jnp.float32),
                pltpu.VMEM((4, depth), jnp.float32),
                pltpu.VMEM((2 * BLOCK, kernels * BLOCK), jnp.bfloat16),
                pltpu.VMEM((BLOCK, depth), jnp.float32),
                pltpu.VMEM((2 * BLOCK, depth), jnp.bfloat16),
                pltpu.VMEM((depth, side), jnp.bfloat16),
                pltpu.VMEM((side + 8, side), jnp.float32),
                pltpu.VMEM((side + 8, side), jnp.float32),
            ],
        ),
        out_shape=[
            jax.ShapeDtypeStruct((exposures, side, side), jnp.float32),
            jax.ShapeDtypeStruct((sky_rows, sky_cols), jnp.bfloat16),
            jax.ShapeDtypeStruct((devices, 8, BLOCK), jnp.float32),
        ],
        compiler_params=pltpu.CompilerParams(vmem_limit_bytes=56 * 1024 * 1024),
        name="convolve",
    )(
        shift_index,
        owners,
        dest_column,
        exposure_weight,
        field_coeffs,
        cutouts,
        horiz_taps,
        vert_taps,
    )

    visits, peers = lax.axis_size("visit"), lax.axis_size("sky")
    pairs = peers // 2
    vmem = pl.BlockSpec(memory_space=pltpu.VMEM)
    piece = (BLOCK, sky_cols)
    tile = (8, BLOCK)

    def sems(*shape):
        return pltpu.SemaphoreType.DMA((2,) + shape)

    strip, sky = pl.pallas_call(
        functools.partial(combine_kernel, visits, pairs),
        in_specs=[
            pl.BlockSpec(memory_space=pl.ANY),
            vmem,
            vmem,
        ],
        out_specs=[vmem, pl.BlockSpec(memory_space=pl.ANY)],
        out_shape=[
            jax.ShapeDtypeStruct(piece, jnp.float32),
            jax.ShapeDtypeStruct((visits, pairs, 2) + piece, jnp.bfloat16),
        ],
        scratch_shapes=[
            pltpu.VMEM((visits, pairs) + piece, jnp.bfloat16),
            pltpu.VMEM((visits, pairs) + piece, jnp.bfloat16),
            pltpu.VMEM((visits, pairs - 1) + piece, jnp.bfloat16),
            pltpu.VMEM((visits - 1,) + piece, jnp.bfloat16),
            pltpu.VMEM((visits - 1,) + piece, jnp.bfloat16),
            pltpu.VMEM((pairs, visits) + tile, jnp.float32),
            pltpu.VMEM((visits, pairs) + tile, jnp.float32),
            pltpu.VMEM((pairs - 1, visits) + tile, jnp.float32),
            pltpu.VMEM((visits,) + tile, jnp.float32),
            pltpu.VMEM((visits - 1,) + tile, jnp.float32),
            pltpu.VMEM((2, TOP, sky_cols), jnp.float32),
            pltpu.VMEM((2, TOP, sky_cols), jnp.float32),
            pltpu.VMEM(piece, jnp.bfloat16),
            pltpu.SemaphoreType.DMA((visits + 1,)),
            sems(visits),
            sems(visits, pairs - 1),
            sems(visits - 1),
            sems(pairs + visits - 1),
            sems(2),
            sems(visits - 1),
            sems(visits, pairs - 1),
            sems(visits, pairs),
        ],
        compiler_params=pltpu.CompilerParams(
            collective_id=0, has_side_effects=True, vmem_limit_bytes=48 * 1024 * 1024
        ),
        name="combine",
    )(
        dense.reshape((visits, pairs, 2) + piece),
        weights.reshape((visits, pairs, 2) + tile),
        threshold_level,
    )
    sky = sky.reshape(sky_rows, sky_cols)

    difference = pl.pallas_call(
        difference_kernel,
        grid_spec=pltpu.PrefetchScalarGridSpec(
            num_scalar_prefetch=2,
            grid=(exposures, tiles),
            in_specs=[
                pl.BlockSpec((1, BLOCK, side), lambda e, p, *_: (e, p, 0)),
                pl.BlockSpec(memory_space=pl.ANY),
            ],
            out_specs=pl.BlockSpec((1, BLOCK, side), lambda e, p, *_: (e, p, 0)),
            scratch_shapes=[
                pltpu.VMEM((exposures, tiles * tiles, BLOCK, BLOCK), jnp.bfloat16),
                pltpu.SemaphoreType.DMA((exposures, tiles * tiles)),
            ],
        ),
        out_shape=jax.ShapeDtypeStruct((exposures, side, side), jnp.float32),
        compiler_params=pltpu.CompilerParams(vmem_limit_bytes=12 * 1024 * 1024),
        name="difference",
    )(owners, dest_column, shifted, sky)
    return (strip, difference)


def solution(mesh):
    placed = (
        P(("visit", "sky"), None, None),
        P(("visit", "sky"), None, None),
        P(("visit", "sky"), None, None),
        P(("visit", "sky"), None, None),
        P(("visit", "sky")),
        P(("visit", "sky"), None, None),
        P(("visit", "sky"), None),
        P(("visit", "sky"), None),
        P(),
    )
    return jax.shard_map(
        shards,
        mesh=mesh,
        in_specs=placed,
        out_specs=(P(("visit", "sky"), None), P(("visit", "sky"), None, None)),
        check_vma=False,
    )
```

```python
import functools
import math
import jax
import jax.numpy as jnp
from jax import lax
from jax.experimental import pallas as pl
from jax.experimental.pallas import tpu as pltpu
from jax.sharding import PartitionSpec as P

BLOCK = 128
PW = 4
SWEEPS = 2
TAIL = 32
TOP = 16

spline_taps = (0.0625, 0.25, 0.375, 0.25, 0.0625)
fine_tau = 0.04
coarse_tau = 0.02


def bf_values(array):
    return array.astype(jnp.bfloat16).astype(jnp.float32)


def conv_kernel(
    shift_ref,
    owner_ref,
    column_ref,
    weight_ref,
    factor_ref,
    x_ref,
    across_ref,
    down_ref,
    shifted_ref,
    dense_ref,
    total_ref,
    padded,
    tap_rows,
    coef,
    across,
    band,
    mixing,
    smeared,
    conv,
    conv_right,
):
    exposure = pl.program_id(0)
    side = x_ref.shape[1]
    tiles = side // BLOCK
    kernels = across_ref.shape[1]
    window = BLOCK + TAIL
    wide = side + BLOCK

    @pl.when(exposure == 0)
    def _():
        dense_ref[...] = jnp.zeros_like(dense_ref)
        total_ref[...] = jnp.zeros_like(total_ref)

    padded[0:TOP, :] = jnp.zeros((TOP, wide), jnp.bfloat16)
    padded[TOP + side : TOP + side + TOP, :] = jnp.zeros((TOP, wide), jnp.bfloat16)
    for t in range(tiles):
        rows = jnp.concatenate(
            [x_ref[0, t * BLOCK : (t + 1) * BLOCK, :], jnp.zeros((BLOCK, BLOCK), jnp.float32)],
            axis=1,
        )
        padded[TOP + t * BLOCK : TOP + (t + 1) * BLOCK, :] = pltpu.roll(rows, 10, 1).astype(
            jnp.bfloat16
        )

    taps = across_ref.shape[2]
    margin = (taps - 1) // 2
    source = lax.broadcasted_iota(jnp.int32, (BLOCK, 2 * BLOCK), 0)
    place = lax.broadcasted_iota(jnp.int32, (BLOCK, 2 * BLOCK), 1)
    backward = (place == lax.rem(2 * BLOCK - source, 2 * BLOCK)) & (source < taps)
    forward = (place == source + (TOP - margin)) & (source < taps)

    def lined(taps_ref, at):
        tap_rows[...] = jnp.zeros_like(tap_rows)
        tap_rows[:, :taps] = taps_ref[0]
        return jnp.dot(
            tap_rows[...].astype(jnp.bfloat16),
            at.astype(jnp.float32).astype(jnp.bfloat16),
            preferred_element_type=jnp.float32,
        )

    across_lines = lined(across_ref, backward)
    down_lines = lined(down_ref, forward)
    quarter_of = lax.broadcasted_iota(jnp.int32, (1, BLOCK), 1) // TAIL
    for j in range(4):
        for k in range(kernels):
            coef[j : j + 1, k * BLOCK : (k + 1) * BLOCK] = jnp.full(
                (1, BLOCK), factor_ref[exposure, j, k]
            )
        for g in range(kernels * TAIL // BLOCK):
            row = jnp.zeros((1, BLOCK), jnp.float32)
            for q in range(BLOCK // TAIL):
                row = jnp.where(
                    quarter_of == q, factor_ref[exposure, j, g * (BLOCK // TAIL) + q], row
                )
            low = kernels * BLOCK + g * BLOCK
            coef[j : j + 1, low : low + BLOCK] = row

    for k in range(kernels):
        line = jnp.broadcast_to(across_lines[k : k + 1, :], (2 * BLOCK, 2 * BLOCK))
        line = pltpu.roll(line, 0, 1, stride=1, stride_axis=0)
        across[:, k * BLOCK : (k + 1) * BLOCK] = line[:, :BLOCK].astype(jnp.bfloat16)
    per = BLOCK // TAIL
    for g in range(kernels // per):
        tail = None
        for q in range(per):
            k = g * per + q
            line = jnp.broadcast_to(down_lines[k : k + 1, :], (BLOCK, 2 * BLOCK))
            line = pltpu.roll(line, 0, 1, stride=1, stride_axis=0)
            band[:, k * BLOCK : (k + 1) * BLOCK] = line[:, :BLOCK]
            part = line[:, BLOCK:]
            if q:
                part = pltpu.roll(part, q * TAIL, 1)
            tail = part if tail is None else tail + part
        first = kernels * BLOCK + g * BLOCK
        band[:, first : first + BLOCK] = tail

    lane = lax.broadcasted_iota(jnp.int32, (1, side), 1).astype(jnp.float32)
    v = (lane + 0.5) / side - 0.5

    def row_tile(t, carry):
        first = pl.multiple_of(t * BLOCK, BLOCK)
        stacked = jnp.concatenate(
            [
                padded[pl.ds(first, window), c * BLOCK : (c + 2) * BLOCK]
                for c in range(tiles)
            ],
            axis=0,
        )
        for pair in range(kernels // 2):
            out = jnp.dot(
                stacked,
                across[:, pair * 2 * BLOCK : (pair + 1) * 2 * BLOCK],
                preferred_element_type=jnp.float32,
            ).astype(jnp.bfloat16)
            for half in range(2):
                k = 2 * pair + half
                for c in range(tiles):
                    piece = out[
                        c * window : (c + 1) * window, half * BLOCK : (half + 1) * BLOCK
                    ]
                    lanes = slice(c * BLOCK, (c + 1) * BLOCK)
                    smeared[k * BLOCK : (k + 1) * BLOCK, lanes] = piece[:BLOCK]
                    low = kernels * BLOCK + k * TAIL
                    smeared[low : low + TAIL, lanes] = piece[BLOCK:]
        row = (first + lax.broadcasted_iota(jnp.int32, (BLOCK, 1), 0)).astype(jnp.float32)
        u = (row + 0.5) / side - 0.5
        depth = band.shape[1]
        step = 4 * BLOCK
        for j in range(depth // step):
            s = slice(j * step, (j + 1) * step)
            b = band[:, s]
            c = coef[:, s]
            mixing[:BLOCK, s] = ((c[0:1] + u * c[1:2]) * b).astype(jnp.bfloat16)
            mixing[BLOCK:, s] = ((c[2:3] + u * c[3:4]) * b).astype(jnp.bfloat16)
        total = jnp.dot(mixing[...], smeared[...], preferred_element_type=jnp.float32)
        value = total[:BLOCK] + v * total[BLOCK:]
        conv[pl.ds(first, BLOCK), :] = value
        moved = pltpu.roll(value, side - 1, 1)
        conv_right[pl.ds(first, BLOCK), :] = jnp.where(
            lax.broadcasted_iota(jnp.int32, (1, side), 1) < side - 1, moved, 0.0
        )
        return carry

    lax.fori_loop(0, tiles, row_tile, 0)
    conv[side : side + 8, :] = jnp.zeros((8, side), jnp.float32)
    conv_right[side : side + 8, :] = jnp.zeros((8, side), jnp.float32)

    def quarter(number):
        return (number.astype(jnp.float32) + 0.5) / 4.0

    weight = bf_values(jnp.full((8, BLOCK), weight_ref[exposure]))
    lanes_of = lax.broadcasted_iota(jnp.int32, (8, BLOCK), 1)
    for p in range(tiles):
        for q in range(tiles):
            b = p * tiles + q
            s = shift_ref[exposure, b]
            fx = quarter(lax.rem(s, 4))
            fy = quarter(lax.div(s, 4))
            r = slice(p * BLOCK, (p + 1) * BLOCK)
            below = slice(p * BLOCK + 1, (p + 1) * BLOCK + 1)
            lanes = slice(q * BLOCK, (q + 1) * BLOCK)
            value = (1.0 - fy) * ((1.0 - fx) * conv[r, lanes] + fx * conv_right[r, lanes]) + fy * (
                (1.0 - fx) * conv[below, lanes] + fx * conv_right[below, lanes]
            )
            shifted_ref[0, r, lanes] = value
            sent = weight[0:1] * value.astype(jnp.bfloat16).astype(jnp.float32)
            at = (
                pl.ds(pl.multiple_of(owner_ref[exposure, b] * BLOCK, BLOCK), BLOCK),
                pl.ds(pl.multiple_of(column_ref[exposure, b] * BLOCK, BLOCK), BLOCK),
            )
            owner = owner_ref[exposure, b]
            total_ref[owner] = total_ref[owner] + jnp.where(
                lanes_of == column_ref[exposure, b], weight, 0.0
            )
            dense_ref[at] = (dense_ref[at].astype(jnp.float32) + sent).astype(jnp.bfloat16)


def difference_kernel(owner_ref, column_ref, shifted_ref, sky_ref, out_ref, blocks, sems):
    exposure, p = pl.program_id(0), pl.program_id(1)
    tiles = shifted_ref.shape[2] // BLOCK
    exposures = owner_ref.shape[0]

    def fetch(e, b):
        source = sky_ref.at[
            pl.ds(pl.multiple_of(owner_ref[e, b] * BLOCK, BLOCK), BLOCK),
            pl.ds(pl.multiple_of(column_ref[e, b] * BLOCK, BLOCK), BLOCK),
        ]
        return pltpu.make_async_copy(source, blocks.at[e, b], sems.at[e, b])

    @pl.when((exposure == 0) & (p == 0))
    def _():
        for e in range(exposures):
            for b in range(tiles * tiles):
                fetch(e, b).start()

    for q in range(tiles):
        b = p * tiles + q
        fetch(exposure, b).wait()
        lanes = slice(q * BLOCK, (q + 1) * BLOCK)
        out_ref[0, :, lanes] = shifted_ref[0, :, lanes] - blocks[exposure, b].astype(jnp.float32)


def grid_of(pairs):
    wide = math.isqrt(pairs)
    if wide * wide != pairs:
        wide = pairs
    return wide, pairs // wide


def spline(values, dilation, axis):
    size = values.shape[axis]
    d = dilation
    near = pltpu.roll(values, d, axis) + pltpu.roll(values, size - d, axis)
    far = pltpu.roll(values, 2 * d, axis) + pltpu.roll(values, size - 2 * d, axis)
    return spline_taps[0] * far + spline_taps[1] * near + spline_taps[2] * values


def shrink(detail, limit):
    return detail - jnp.minimum(jnp.maximum(detail, -limit), limit)


def smooth(values, dilation):
    rows, cols = values.shape
    down = spline(values, dilation, 0)
    wide = jnp.concatenate([down, jnp.zeros((rows, BLOCK), jnp.float32)], axis=1)
    return spline(wide, dilation, 1)[:, :cols]


def combine_kernel(
    visits,
    pairs,
    dense_ref,
    weight_ref,
    level_ref,
    strip_ref,
    sky_ref,
    held,
    part,
    from_twin,
    from_first,
    middle,
    from_second,
    going,
    from_visit,
    w_part,
    w_twin,
    w_plane,
    w_going,
    w_visit,
    edges,
    halo,
    template,
    local_sem,
    twin_sem,
    first_sem,
    second_sem,
    visit_sem,
    w_sem,
    halo_sem,
    back_visit_sem,
    back_first_sem,
    back_second_sem,
    back_twin_sem,
):
    z = lax.axis_index("visit")
    sky = lax.axis_index("sky")
    peers = 2 * pairs
    devices = visits * peers
    p, core = lax.div(sky, 2), lax.rem(sky, 2)
    me = z * peers + sky
    other = 1 - core

    def linear(number):
        return (lax.div(number, peers), lax.rem(number, peers))

    twin = (z, p * 2 + other)
    places = [lax.rem(p + o, pairs) for o in range(1, pairs)]
    plane = [(z, place * 2 + core) for place in places]
    heights = [lax.rem(z + d, visits) for d in range(1, visits)]
    column = [(height, sky) for height in heights]
    ring = [linear(lax.rem(me + devices - 1, devices)), linear(lax.rem(me + 1, devices))]

    wide, tall = grid_of(pairs)
    y, x = lax.div(p, wide), lax.rem(p, wide)
    along = [
        [(z, (y * wide + lax.rem(x + o, wide)) * 2 + core) for o in range(1, wide)],
        [(z, (lax.rem(y + o, tall) * wide + x) * 2 + core) for o in range(1, tall)],
    ]
    sizes, spots = (wide, tall), (x, y)
    half = strip_ref.shape[1] // 2

    everyone = [twin] + plane + column + ring
    barrier = pltpu.get_barrier_semaphore()
    for peer in everyone:
        pl.semaphore_signal(
            barrier, inc=1, device_id=peer, device_id_type=pl.DeviceIdType.MESH
        )
    pl.semaphore_wait(barrier, len(everyone))

    def send(src, dst, sems, index, peer):
        copy = pltpu.make_async_remote_copy(
            src_ref=src,
            dst_ref=dst,
            send_sem=sems.at[(0,) + index],
            recv_sem=sems.at[(1,) + index],
            device_id=peer,
            device_id_type=pl.DeviceIdType.MESH,
        )
        copy.start()
        sent.append(copy)
        return copy

    sent = []
    order = heights + [z]
    w_copy = send(weight_ref.at[:, :, other], w_twin, w_sem, (0,), twin)
    local, across = [], []
    for j, height in enumerate(order):
        across.append(
            send(dense_ref.at[height, :, other], from_twin.at[j], twin_sem, (j,), twin)
        )
        own = pltpu.make_async_copy(dense_ref.at[height, :, core], held.at[j], local_sem.at[j])
        own.start()
        local.append(own)

    w_copy.wait_recv()
    for height in range(visits):
        for place in range(pairs):
            w_part[place, height] = weight_ref[height, place, core] + w_twin[height, place]
    w_copies = [
        send(w_part.at[place], w_plane.at[o], w_sem, (1 + o,), plane[o])
        for o, place in enumerate(places)
    ]

    def spread(j):
        local[j].wait()
        across[j].wait_recv()

        def add(place, carry):
            total = (
                held[j, place].astype(jnp.float32) + from_twin[j, place].astype(jnp.float32)
            ).astype(jnp.bfloat16)
            part[j, 0, lax.rem(place, wide) * tall + lax.div(place, wide)] = total[:, :half]
            part[j, 1, place] = total[:, half:]
            return carry

        lax.fori_loop(0, pairs, add, 0)
        copies = []
        for h in range(2):
            first, second = sizes[h], sizes[1 - h]
            for o in range(1, first):
                at = pl.ds(lax.rem(spots[h] + o, first) * second, second)
                copies.append(
                    send(
                        part.at[j, h, at],
                        from_first.at[j, h, o - 1],
                        first_sem,
                        (j, h, o - 1),
                        along[h][o - 1],
                    )
                )
        return copies

    def line(j, h, spot):
        first, second = sizes[h], sizes[1 - h]
        total = part[j, h, spots[h] * second + spot].astype(jnp.float32)
        for o in range(first - 1):
            total = total + from_first[j, h, o, spot].astype(jnp.float32)
        return total

    def turn(j):
        copies = []
        for copy in moves[j]:
            copy.wait_recv()
        for h in range(2):
            second = sizes[1 - h]
            for o in range(1, second):
                spot = lax.rem(spots[1 - h] + o, second)
                middle[j, h, o - 1] = line(j, h, spot).astype(jnp.bfloat16)
                copies.append(
                    send(
                        middle.at[j, h, o - 1],
                        from_second.at[j, h, o - 1],
                        second_sem,
                        (j, h, o - 1),
                        along[1 - h][o - 1],
                    )
                )
        return copies

    def gathered(j):
        for copy in turns[j]:
            copy.wait_recv()
        halves = []
        for h in range(2):
            total = line(j, h, spots[1 - h])
            for o in range(sizes[1 - h] - 1):
                total = total + from_second[j, h, o].astype(jnp.float32)
            halves.append(total)
        return jnp.concatenate(halves, axis=1)

    moves = [spread(0)]
    for copy in w_copies:
        copy.wait_recv()
    w_total = w_part[p]
    for o in range(pairs - 1):
        w_total = w_total + w_plane[o]
    w_going[...] = w_total
    w_copies = [
        send(w_going.at[height], w_visit.at[j], w_sem, (pairs + j,), column[j])
        for j, height in enumerate(heights)
    ]
    climbs, turns = [], []
    for j in range(1, visits + 2):
        if j < visits:
            moves.append(spread(j))
        if j <= visits:
            turns.append(turn(j - 1))
        if j >= 2:
            i = j - 2
            if i < visits - 1:
                going[i] = gathered(i).astype(jnp.bfloat16)
                climbs.append(send(going.at[i], from_visit.at[i], visit_sem, (i,), column[i]))
    weight = w_going[z]
    for copy, j in zip(w_copies, range(visits - 1)):
        copy.wait_recv()
        weight = weight + w_visit[j]
    total = gathered(visits - 1)
    for copy, j in zip(climbs, range(visits - 1)):
        copy.wait_recv()
        total = total + from_visit[j].astype(jnp.float32)
    cols = total.shape[1]
    blocks = cols // BLOCK
    scale = jnp.concatenate(
        [jnp.broadcast_to(1.0 + weight[0:1, c : c + 1], (1, BLOCK)) for c in range(blocks)], axis=1
    )
    coadd = total / scale
    edges[0] = coadd[:TOP]
    edges[1] = coadd[BLOCK - TOP :]
    shifts = [
        send(edges.at[0], halo.at[1], halo_sem, (0,), ring[0]),
        send(edges.at[1], halo.at[0], halo_sem, (1,), ring[1]),
    ]
    for copy in shifts:
        copy.wait_recv()

    rows = BLOCK + 2 * TOP
    position = me * BLOCK - TOP + lax.broadcasted_iota(jnp.int32, (rows, 1), 0)
    inside = jnp.where((position >= 0) & (position < devices * BLOCK), 1.0, 0.0)
    above, below = jnp.maximum(me - 1, 0), jnp.minimum(me + 1, devices - 1)

    def levels(owner, height):
        row = level_ref[pl.ds(owner, 1), :].astype(jnp.float32)
        return jnp.concatenate(
            [
                jnp.broadcast_to(row[:, c : c + 1], (height, BLOCK))
                for c in range(blocks)
            ],
            axis=1,
        )

    limits = jnp.concatenate([levels(above, TOP), levels(me, BLOCK), levels(below, TOP)], axis=0)
    values = jnp.concatenate([halo[0], coadd, halo[1]], axis=0)
    for _ in range(SWEEPS):
        values = values * inside
        fine = smooth(values, 1) * inside
        coarse = smooth(fine, 2)
        values = (
            coarse
            + shrink(values - fine, fine_tau * limits)
            + shrink(fine - coarse, coarse_tau * limits)
        )
    strip = values[TOP : TOP + BLOCK]
    strip_ref[...] = strip
    template[...] = strip.astype(jnp.bfloat16)

    mine = sky_ref.at[z, p, core]
    own = pltpu.make_async_copy(template, mine, local_sem.at[visits])
    own.start()
    climbs = [
        send(template, mine, back_visit_sem, (d,), column[d]) for d in range(visits - 1)
    ]
    spreads, onward, twins = [], [], []

    def chunk(d, h, row, col):
        owner = lax.rem(row, tall) * wide + lax.rem(col, wide)
        return sky_ref.at[
            lax.rem(z + visits - d, visits), owner, core, :, pl.ds(h * half, half)
        ]

    def away(d, h, i, o):
        steps = [(x, y), (y, x)][h]
        one, two = steps[0] + sizes[h] - i, steps[1] + sizes[1 - h] - o
        return chunk(d, h, two, one) if h == 0 else chunk(d, h, one, two)

    def second_leg(d, h, i, source, place):
        onward.append(
            [
                (d, h, i, o, send(source, place, back_second_sem, (d, h, i, o - 1), along[1 - h][o - 1]))
                for o in range(1, sizes[1 - h])
            ]
        )

    def outward(d):
        if d > 0:
            climbs[d - 1].wait_recv()
        batch = []
        for h in range(2):
            place = away(d, h, 0, 0)
            source = template.at[:, pl.ds(h * half, half)] if d == 0 else place
            for o in range(1, sizes[h]):
                batch.append(
                    (h, o, send(source, place, back_first_sem, (d, h, o - 1), along[h][o - 1]))
                )
        for h in range(2):
            place = away(d, h, 0, 0)
            source = template.at[:, pl.ds(h * half, half)] if d == 0 else place
            second_leg(d, h, 0, source, place)
            twins.append(send(source, place, back_twin_sem, (d, h, 0, 0), twin))
        spreads.append(batch)

    def forward(number):
        for d, h, i, o, copy in onward[number]:
            copy.wait_recv()
            place = away(d, h, i, o)
            twins.append(send(place, place, back_twin_sem, (d, h, i, o), twin))

    outward(0)
    ready = 0
    for d in range(visits):
        if d + 1 < visits:
            outward(d + 1)
        stop = len(onward)
        for h, i, copy in spreads[d]:
            copy.wait_recv()
            place = away(d, h, i, 0)
            second_leg(d, h, i, place, place)
            twins.append(send(place, place, back_twin_sem, (d, h, i, 0), twin))
        if d > 0:
            while ready < stop:
                forward(ready)
                ready += 1
    while ready < len(onward):
        forward(ready)
        ready += 1
    for copy in twins:
        copy.wait_recv()
    own.wait()
    for copy in sent:
        copy.wait_send()


def shards(
    cutouts,
    vert_taps,
    horiz_taps,
    field_coeffs,
    exposure_weight,
    dest_owner,
    dest_column,
    shift_index,
    threshold_level,
):
    exposures, side, _ = cutouts.shape
    tiles = side // BLOCK
    kernels, taps = vert_taps.shape[1:]
    axes = ("visit", "sky")
    devices = lax.axis_size("visit") * lax.axis_size("sky")
    sky_rows = devices * BLOCK
    sky_cols = PW * BLOCK
    owners = dest_owner.reshape(exposures, tiles * tiles)

    depth = kernels * (BLOCK + TAIL)
    shifted, dense, weights = pl.pallas_call(
        conv_kernel,
        grid_spec=pltpu.PrefetchScalarGridSpec(
            num_scalar_prefetch=5,
            grid=(exposures,),
            in_specs=[
                pl.BlockSpec((1, side, side), lambda e, *_: (e, 0, 0)),
                pl.BlockSpec((1, kernels, taps), lambda e, *_: (e, 0, 0)),
                pl.BlockSpec((1, kernels, taps), lambda e, *_: (e, 0, 0)),
            ],
            out_specs=[
                pl.BlockSpec((1, side, side), lambda e, *_: (e, 0, 0)),
                pl.BlockSpec((sky_rows, sky_cols), lambda e, *_: (0, 0)),
                pl.BlockSpec((devices, 8, BLOCK), lambda e, *_: (0, 0, 0)),
            ],
            scratch_shapes=[
                pltpu.VMEM((side + 2 * TOP, side + BLOCK), jnp.bfloat16),
                pltpu.VMEM((kernels, BLOCK), jnp.float32),
                pltpu.VMEM((4, depth), jnp.float32),
                pltpu.VMEM((2 * BLOCK, kernels * BLOCK), jnp.bfloat16),
                pltpu.VMEM((BLOCK, depth), jnp.float32),
                pltpu.VMEM((2 * BLOCK, depth), jnp.bfloat16),
                pltpu.VMEM((depth, side), jnp.bfloat16),
                pltpu.VMEM((side + 8, side), jnp.float32),
                pltpu.VMEM((side + 8, side), jnp.float32),
            ],
        ),
        out_shape=[
            jax.ShapeDtypeStruct((exposures, side, side), jnp.float32),
            jax.ShapeDtypeStruct((sky_rows, sky_cols), jnp.bfloat16),
            jax.ShapeDtypeStruct((devices, 8, BLOCK), jnp.float32),
        ],
        compiler_params=pltpu.CompilerParams(vmem_limit_bytes=56 * 1024 * 1024),
        name="convolve",
    )(
        shift_index,
        owners,
        dest_column,
        exposure_weight,
        field_coeffs,
        cutouts,
        horiz_taps,
        vert_taps,
    )

    visits, peers = lax.axis_size("visit"), lax.axis_size("sky")
    pairs = peers // 2
    vmem = pl.BlockSpec(memory_space=pltpu.VMEM)
    piece = (BLOCK, sky_cols)
    tile = (8, BLOCK)
    halved = (BLOCK, sky_cols // 2)
    most, least = max(grid_of(pairs)), min(grid_of(pairs))

    def sems(*shape):
        return pltpu.SemaphoreType.DMA((2,) + shape)

    strip, sky = pl.pallas_call(
        functools.partial(combine_kernel, visits, pairs),
        in_specs=[
            pl.BlockSpec(memory_space=pl.ANY),
            vmem,
            vmem,
        ],
        out_specs=[vmem, pl.BlockSpec(memory_space=pl.ANY)],
        out_shape=[
            jax.ShapeDtypeStruct(piece, jnp.float32),
            jax.ShapeDtypeStruct((visits, pairs, 2) + piece, jnp.bfloat16),
        ],
        scratch_shapes=[
            pltpu.VMEM((visits, pairs) + piece, jnp.bfloat16),
            pltpu.VMEM((visits, 2, pairs) + halved, jnp.bfloat16),
            pltpu.VMEM((visits, pairs) + piece, jnp.bfloat16),
            pltpu.VMEM((visits, 2, most - 1, least) + halved, jnp.bfloat16),
            pltpu.VMEM((visits, 2, most - 1) + halved, jnp.bfloat16),
            pltpu.VMEM((visits, 2, most - 1) + halved, jnp.bfloat16),
            pltpu.VMEM((visits - 1,) + piece, jnp.bfloat16),
            pltpu.VMEM((visits - 1,) + piece, jnp.bfloat16),
            pltpu.VMEM((pairs, visits) + tile, jnp.float32),
            pltpu.VMEM((visits, pairs) + tile, jnp.float32),
            pltpu.VMEM((pairs - 1, visits) + tile, jnp.float32),
            pltpu.VMEM((visits,) + tile, jnp.float32),
            pltpu.VMEM((visits - 1,) + tile, jnp.float32),
            pltpu.VMEM((2, TOP, sky_cols), jnp.float32),
            pltpu.VMEM((2, TOP, sky_cols), jnp.float32),
            pltpu.VMEM(piece, jnp.bfloat16),
            pltpu.SemaphoreType.DMA((visits + 1,)),
            sems(visits),
            sems(visits, 2, most - 1),
            sems(visits, 2, most - 1),
            sems(visits - 1),
            sems(pairs + visits - 1),
            sems(2),
            sems(visits - 1),
            sems(visits, 2, most - 1),
            sems(visits, 2, most, most - 1),
            sems(visits, 2, most, most),
        ],
        compiler_params=pltpu.CompilerParams(
            collective_id=0, has_side_effects=True, vmem_limit_bytes=48 * 1024 * 1024
        ),
        name="combine",
    )(
        dense.reshape((visits, pairs, 2) + piece),
        weights.reshape((visits, pairs, 2) + tile),
        threshold_level,
    )
    sky = sky.reshape(sky_rows, sky_cols)

    difference = pl.pallas_call(
        difference_kernel,
        grid_spec=pltpu.PrefetchScalarGridSpec(
            num_scalar_prefetch=2,
            grid=(exposures, tiles),
            in_specs=[
                pl.BlockSpec((1, BLOCK, side), lambda e, p, *_: (e, p, 0)),
                pl.BlockSpec(memory_space=pl.ANY),
            ],
            out_specs=pl.BlockSpec((1, BLOCK, side), lambda e, p, *_: (e, p, 0)),
            scratch_shapes=[
                pltpu.VMEM((exposures, tiles * tiles, BLOCK, BLOCK), jnp.bfloat16),
                pltpu.SemaphoreType.DMA((exposures, tiles * tiles)),
            ],
        ),
        out_shape=jax.ShapeDtypeStruct((exposures, side, side), jnp.float32),
        compiler_params=pltpu.CompilerParams(vmem_limit_bytes=12 * 1024 * 1024),
        name="difference",
    )(owners, dest_column, shifted, sky)
    return (strip, difference)


def solution(mesh):
    placed = (
        P(("visit", "sky"), None, None),
        P(("visit", "sky"), None, None),
        P(("visit", "sky"), None, None),
        P(("visit", "sky"), None, None),
        P(("visit", "sky")),
        P(("visit", "sky"), None, None),
        P(("visit", "sky"), None),
        P(("visit", "sky"), None),
        P(),
    )
    return jax.shard_map(
        shards,
        mesh=mesh,
        in_specs=placed,
        out_specs=(P(("visit", "sky"), None), P(("visit", "sky"), None, None)),
        check_vma=False,
    )
```
